512 devices in a mesh: grid: 64 (over x, z, core), mem: 8 (over y).
Axes of the slice: x: 4, y: 8, z: 8, core: 2. Of those that a mesh axis runs over, the one named last changes fastest.
Arguments:
- ens: bfloat16 [80, 4, 32, 65536], P('mem', None, None, 'grid'), may hold values from -6 to 6
- control: float32 [4, 32, 65536], P(None, None, 'grid'), may hold values from -6 to 6
- col_count: int32 [512], P('grid'), may hold values from 64 to 128, as said below
- level_index: int32 [32], replicated, may hold values from 43 to 136, as said below
- pair_blocks: int32 [6144, 2], P('grid'), may hold values from 0 to 511, as said below
- loc_blocks: bfloat16 [6144, 128, 128], P('grid'), may hold values from -0.109375 to 0.109375
Outputs:
- mixed: float32 [4, 32, 65536], P(None, None, ('grid', 'mem'))
The draws below stay inside these ranges and needn't reach their ends.
Inputs may be any that keep to these rules, and one draw needn't show every extreme that they name: `pair_blocks`: rows come in groups of 12, one group for each block b in order; group b holds the pairs (b, (b + k) mod 512) for k = 0, k = 12 and 10 further distinct k between 1 and 11. `col_count`: some block is full. `level_index`: strictly increasing by steps of 1 to 3; the last is 136.
All inputs are finite; a program needn't handle non-finite values.
Results may differ from the reference program's by a relative error of at most 0.0029.
Values may be sent and summed in bfloat16 or wider, within the bound.
No kernel may reach another device: no remote copies, remote signals or barrier semaphores. Data moves between devices by JAX's collectives and lax.ppermute only.
A program may use at most 64 MiB of HBM per device.

```python
import jax
import jax.numpy as jnp
from jax import lax

BLOCK = 128
LEV = 32
SLOTS = 4
PER = 12
SPAN = 12
MEMBERS = 80
BLOCKS = 512
COLUMNS = 65536


def draw_col_count(key, part):
    key = jax.random.fold_in(key, 11)
    count_key, full_key = jax.random.split(key)
    counts = jax.random.randint(count_key, (BLOCKS,), BLOCK // 2, BLOCK + 1)
    full = jax.random.randint(full_key, (), 0, BLOCKS)
    return jnp.where(jnp.arange(BLOCKS) == full, BLOCK, counts).astype(jnp.int32)


def draw_level_index(key, part):
    key = jax.random.fold_in(key, 12)
    steps = jax.random.randint(key, (LEV,), 1, 4)
    tail = jnp.cumsum(steps[::-1])[::-1] - steps
    return (136 - tail).astype(jnp.int32)


def draw_pair_blocks(key, part):
    key = jax.random.fold_in(key, 13)
    block_keys = jax.random.split(key, BLOCKS)
    picked = jax.vmap(lambda k: jax.random.permutation(k, SPAN - 1)[:PER - 2] + 1)(block_keys)
    fixed = jnp.broadcast_to(jnp.array([0, SPAN], jnp.int32), (BLOCKS, 2))
    offsets = jnp.concatenate([fixed, picked.astype(jnp.int32)], axis=1)
    first = jnp.broadcast_to(jnp.arange(BLOCKS, dtype=jnp.int32)[:, None], (BLOCKS, PER))
    second = (first + offsets) % BLOCKS
    return jnp.stack([first, second], axis=-1).reshape(BLOCKS * PER, 2).astype(jnp.int32)


def steps_of(own_key, shape, cuts, low, largest):
    def one(axis_at, parts):
        heights = jax.random.uniform(jax.random.fold_in(jax.random.fold_in(own_key, 6), axis_at), (parts,), jnp.float32, low / len(cuts), largest / len(cuts))
        return jnp.repeat(jnp.exp(heights), shape[axis_at] // parts).reshape((-1,) + (1,) * (len(shape) - axis_at - 1))

    gain = one(*cuts[0])
    for cut in cuts[1:]:
        gain = gain * one(*cut)
    return gain


def centred(rng, extent, scale, reach, cuts=(), held_as=jnp.bfloat16):
    result = jax.random.normal(rng, extent, jnp.float32) * scale
    if len(cuts) > 0:
        result = steps_of(rng, extent, cuts, -0.22, 0.18) * result
    return jnp.clip(result, min=-reach, max=reach).astype(held_as)


def setup_inputs(seed: int = 0) -> dict:
    key_list = jax.random.split(jax.random.key(seed), 7)
    return {
        "ens": centred(key_list[0], (MEMBERS, SLOTS, LEV, COLUMNS), 1.0, 6.0, ((0, 8), (3, 64))),
        "control": centred(key_list[1], (SLOTS, LEV, COLUMNS), 1.0, 6.0, ((2, 64),), jnp.float32),
        "col_count": draw_col_count(jax.random.fold_in(key_list[6], 71), 0),
        "level_index": draw_level_index(jax.random.fold_in(key_list[6], 71), 0),
        "pair_blocks": draw_pair_blocks(jax.random.fold_in(key_list[6], 71), 0),
        "loc_blocks": centred(key_list[5], (BLOCKS * PER, BLOCK, BLOCK), (256 * PER) ** -0.5, 0.109375, ((0, 64),)),
    }


vertical_scale = 8.0


def reference(ens, control, col_count, level_index, pair_blocks, loc_blocks):
    columns = jnp.arange(BLOCKS * BLOCK)
    live = ((columns % BLOCK) < jnp.repeat(col_count, BLOCK)).astype(jnp.float32)
    masked = control * live
    levels = level_index.astype(jnp.float32)
    vert = jnp.exp(-jnp.abs(levels[:, None] - levels[None, :]) / vertical_scale)

    def one_member(member):
        weighted = jnp.sum(member.astype(jnp.float32) * masked, axis=0)
        return jnp.dot(vert, weighted, precision=lax.Precision.HIGHEST).astype(jnp.bfloat16)

    lifted = lax.map(one_member, ens)
    by_block = lifted.reshape(MEMBERS, LEV, BLOCKS, BLOCK).transpose(2, 0, 1, 3)
    pairs = pair_blocks.reshape(BLOCKS, PER, 2)
    locs = loc_blocks.reshape(BLOCKS, PER, BLOCK, BLOCK)

    def step(spread, item):
        group, local_loc = item
        first_rows = by_block[group[:, 0]].astype(jnp.float32)
        second_rows = by_block[group[:, 1]].astype(jnp.float32)
        loc_wide = local_loc.astype(jnp.float32)
        to_first = jnp.einsum("pab,pmlb->pmla", loc_wide, second_rows)
        apart = (group[:, 0] != group[:, 1]).astype(jnp.float32)
        to_second = jnp.einsum("pab,pmla->pmlb", loc_wide, first_rows) * apart[:, None, None, None]
        spread = spread.at[group[:, 0]].add(to_first)
        spread = spread.at[group[:, 1]].add(to_second)
        return spread, None

    start = jnp.zeros((BLOCKS, MEMBERS, LEV, BLOCK), jnp.float32)
    spread, unused = lax.scan(step, start, (pairs, locs))
    spread_cols = spread.transpose(1, 2, 0, 3).reshape(MEMBERS, LEV, BLOCKS * BLOCK)

    def add_member(total, item):
        member, member_spread = item
        return total + member.astype(jnp.float32) * member_spread[None], None

    total, unused = lax.scan(add_member, jnp.zeros((SLOTS, LEV, BLOCKS * BLOCK), jnp.float32), (ens, spread_cols))
    return total * live / (MEMBERS - 1)
```

```python
import functools

import jax
import jax.numpy as jnp
from jax import lax
from jax.experimental import pallas as pl
from jax.experimental.pallas import tpu as pltpu
from jax.sharding import PartitionSpec as P

SPAN = 12
WIDTH = 128
DEV = 8
TWO = 2 * WIDTH
LANES = 16 * WIDTH

vertical_scale = 8.0

F32 = jnp.float32
BF16 = jnp.bfloat16
SMEM = pl.BlockSpec(memory_space=pltpu.SMEM)


def dot(a, b):
    return lax.dot_general(a, b, (((1,), (0,)), ((), ())), preferred_element_type=F32)


def dot_t(a, b):
    return lax.dot_general(a, b, (((1,), (1,)), ((), ())), preferred_element_type=F32)


def is_odd(pairs_ref):
    return lax.rem(pairs_ref[0, 0] // DEV, 2) == 1


def fill_band(pairs_ref, loc_ref, g, per, blocks, store):
    zero = jnp.zeros((WIDTH, WIDTH), BF16)
    store(0, SPAN + 1, zero)
    store(1, 0, zero)
    for ii in range(2):
        left = SPAN * (SPAN + 1) // 2
        for p in range(per):
            at = (2 * g + ii) * per + p
            k = pairs_ref[1, at] - pairs_ref[0, at]
            k = jnp.where(k < 0, k + blocks, k)
            left = left - k
            store(ii, k + ii, loc_ref[ii * per + p])
        store(ii, left + ii, zero)


def lift_kernel(members, slots, levels, per, blocks, pairs_ref, count_ref, level_ref, ens_ref, control_ref, loc_ref,
                own_ref, pay1_ref, pay3_ref, mrg_ref, lifted, band, vert):
    g = pl.program_id(0)
    odd = is_odd(pairs_ref)
    group = WIDTH // levels

    @pl.when(g == 0)
    def _():
        lane = lax.broadcasted_iota(jnp.int32, (levels, WIDTH), 1)
        row = lax.broadcasted_iota(jnp.int32, (levels, WIDTH), 0)
        by_lane = jnp.zeros((levels, WIDTH), F32)
        by_row = jnp.zeros((levels, WIDTH), F32)
        for l in range(levels):
            value = level_ref[l].astype(F32)
            by_lane = jnp.where(lane % levels == l, value, by_lane)
            by_row = jnp.where(row == l, value, by_row)
        v = jnp.exp(-jnp.abs(by_row - by_lane) / vertical_scale)
        for q in range(group):
            part = jnp.where(lane // levels == q, v, 0.0)
            high = part.astype(BF16)
            vert[0, q * levels:(q + 1) * levels, :] = high
            vert[1, q * levels:(q + 1) * levels, :] = (part - high.astype(F32)).astype(BF16)

    lane = lax.broadcasted_iota(jnp.int32, (levels, TWO), 1)
    used = lane < jnp.where(lane < WIDTH, count_ref[2 * g], WIDTH + count_ref[2 * g + 1])
    masked = [jnp.where(used, control_ref[t], 0.0) for t in range(slots)]
    for m0 in range(0, members, group):
        some = min(group, members - m0)
        n = some * levels
        rows = []
        for m in range(m0, m0 + some):
            w = ens_ref[m, 0].astype(F32) * masked[0]
            for t in range(1, slots):
                w = w + ens_ref[m, t].astype(F32) * masked[t]
            rows.append(w)
        w = jnp.concatenate(rows, axis=0)
        high = w.astype(BF16)
        low = (w - high.astype(F32)).astype(BF16)
        vh = vert[0, :n, :n]
        vl = vert[1, :n, :n]
        out = (dot(vh, low) + dot(vl, high) + dot(vh, high)).astype(BF16)
        at = pl.ds(m0 * levels, n)
        lifted[at, pl.ds(pl.multiple_of(g * TWO, TWO), TWO)] = out
        own_ref[at, :] = out

        @pl.when(odd)
        def _():
            pay3_ref[2 * g, at, :] = out[:, :WIDTH]
            pay3_ref[2 * g + 1, at, :] = out[:, WIDTH:]

        @pl.when(jnp.logical_not(odd))
        def _():
            pay1_ref[2 * g, at, :] = out[:, :WIDTH]
            pay1_ref[2 * g + 1, at, :] = out[:, WIDTH:]

    def store(ii, offset, value):
        row = pl.multiple_of(g * TWO + ii * WIDTH, WIDTH)
        col = pl.multiple_of((2 * g + offset) * WIDTH, WIDTH)
        band[pl.ds(row, WIDTH), pl.ds(col, WIDTH)] = value

    fill_band(pairs_ref, loc_ref, g, per, blocks, store)

    @pl.when(g == DEV // 2 - 1)
    def _():
        for q in range(DEV, DEV + SPAN, 2):
            first = max(0, q - SPAN) * WIDTH
            c = dot(lifted[:, first:], band[first:, q * WIDTH:(q + 2) * WIDTH])
            cb = c.astype(BF16)

            @pl.when(odd)
            def _():
                for e in range(2):
                    if q < 12:
                        mrg_ref[q - 8 + e] = c[:, e * WIDTH:(e + 1) * WIDTH]
                    else:
                        pay1_ref[(q - 8 if q < 16 else q - 16) + e] = cb[:, e * WIDTH:(e + 1) * WIDTH]

            @pl.when(jnp.logical_not(odd))
            def _():
                for e in range(2):
                    pay3_ref[q - 8 + e] = cb[:, e * WIDTH:(e + 1) * WIDTH]


def near_kernel(per, blocks, pairs_ref, loc_ref, own_ref, acc_ref, band_ref):
    step = pl.program_id(0)

    def store(ii, offset, value):
        col = pl.multiple_of((offset + 2) * WIDTH, WIDTH)
        band_ref[0, ii * WIDTH:(ii + 1) * WIDTH, pl.ds(col, WIDTH)] = value

    fill_band(pairs_ref, loc_ref, step, per, blocks, store)
    for g in range(DEV // 2):
        @pl.when(step == g)
        def _():
            c0 = g * TWO
            mine = own_ref[:, c0:c0 + TWO]
            to_first = dot_t(own_ref[:, c0:], band_ref[0, :, TWO:TWO + DEV * WIDTH - c0])
            cross = dot(mine[:, :WIDTH], band_ref[0, :WIDTH, TWO + WIDTH:2 * TWO])
            if g == 0:
                acc_ref[:, :WIDTH] = to_first[:, :WIDTH]
                acc_ref[:, WIDTH:TWO] = to_first[:, WIDTH:] + cross
            else:
                acc_ref[:, c0:c0 + WIDTH] += to_first[:, :WIDTH]
                acc_ref[:, c0 + WIDTH:c0 + TWO] += to_first[:, WIDTH:] + cross
            if g < DEV // 2 - 1:
                to_second = dot(mine, band_ref[0, :, 2 * TWO:TWO + DEV * WIDTH - c0])
                if g == 0:
                    acc_ref[:, TWO:] = to_second
                else:
                    acc_ref[:, c0 + TWO:] += to_second


def merge_kernel(pairs_ref, mrg_ref, head_ref, tail_ref, out_ref):
    odd = is_odd(pairs_ref)

    @pl.when(odd)
    def _():
        out_ref[...] = (mrg_ref[...] + tail_ref[...].astype(F32)).astype(BF16)

    @pl.when(jnp.logical_not(odd))
    def _():
        out_ref[...] = head_ref[...]


def far_kernel(pairs_ref, r1_ref, r3_ref, band_ref, acc_ref, out_ref, far):
    step = pl.program_id(0)
    odd = is_odd(pairs_ref)

    @pl.when(jnp.logical_and(step == 0, odd))
    def _():
        for b in range(DEV):
            far[:, b * WIDTH:(b + 1) * WIDTH] = r1_ref[b]

    @pl.when(jnp.logical_and(step == 0, jnp.logical_not(odd)))
    def _():
        for b in range(DEV):
            far[:, b * WIDTH:(b + 1) * WIDTH] = r3_ref[b]

    for g in range(DEV // 2):
        @pl.when(step == g)
        def _():
            last = min(DEV, 2 * g + SPAN + 2 - DEV)
            start = (DEV - 2 * g + 2) * WIDTH
            out_ref[...] = acc_ref[...] + dot_t(far[:, :last * WIDTH], band_ref[0, :, start:start + last * WIDTH])


def mix_kernel(members, slots, levels, members_all, pairs_ref, count_ref, ens_ref, acc_ref, band_ref, r1_ref, r3_ref,
               r1b_ref, r3b_ref, out_ref, spread):
    g = pl.program_id(0)
    odd = is_odd(pairs_ref)
    even = jnp.logical_not(odd)
    spread[...] = acc_ref[...]

    @pl.when(g >= 2)
    def _():
        def add2(x_ref):
            for e in range(2):
                spread[...] += dot_t(x_ref[e], band_ref[0, :, (e + 2) * WIDTH:(e + 3) * WIDTH])

        def add4(x_ref):
            for e in range(4):
                spread[...] += dot_t(x_ref[e], band_ref[0, :, e * WIDTH:(e + 1) * WIDTH])

        for flag, ref in ((odd, r1b_ref), (even, r3b_ref)):
            @pl.when(jnp.logical_and(flag, g == 2))
            def _():
                add2(ref)

            @pl.when(jnp.logical_and(flag, g == 3))
            def _():
                add4(ref)

    for e in range(2):
        cols = pl.ds(e * WIDTH, WIDTH)

        @pl.when(odd)
        def _():
            spread[:, cols] += r3_ref[e].astype(F32)

        @pl.when(jnp.logical_and(odd, g < 2))
        def _():
            spread[:, cols] += r3b_ref[2 * jnp.minimum(g, 1) + e].astype(F32)

        @pl.when(jnp.logical_and(even, g < 2))
        def _():
            spread[:, cols] += r1b_ref[2 * jnp.minimum(g, 1) + e].astype(F32)

        @pl.when(jnp.logical_and(even, g >= 2))
        def _():
            spread[:, cols] += r1_ref[e].astype(F32)

    lane = lax.broadcasted_iota(jnp.int32, (levels, WIDTH), 1)
    for e in range(2):
        cols = pl.ds(e * WIDTH, WIDTH)
        used = lane < count_ref[2 * g + e]
        totals = [jnp.zeros((levels, WIDTH), F32) for _ in range(slots)]
        for m in range(members):
            s = spread[m * levels:(m + 1) * levels, cols]
            for t in range(slots):
                totals[t] = totals[t] + ens_ref[m, t, :, cols].astype(F32) * s
        for t in range(slots):
            out_ref[e, t] = jnp.where(used, totals[t] / (members_all - 1), 0.0).astype(BF16)


def params(mib):
    return pltpu.CompilerParams(vmem_limit_bytes=mib << 20, dimension_semantics=("arbitrary",))


def per_device(ens, control, col_count, level_index, pair_blocks, loc_blocks):
    blocks_dev = col_count.shape[0]
    per = pair_blocks.shape[0] // blocks_dev
    peers = lax.axis_size("grid")
    blocks = peers * blocks_dev
    members, slots, levels, columns = ens.shape
    members_all = members * lax.axis_size("mem")
    rows = members * levels
    assert blocks_dev == DEV and columns == DEV * WIDTH and per == SPAN and peers % 2 == 0
    pairs = pair_blocks.T
    steps = DEV // 2
    one = lambda shape: pl.BlockSpec(shape, lambda g: (0,) * len(shape))
    ens_spec = pl.BlockSpec((members, slots, levels, TWO), lambda g: (0, 0, 0, g))
    loc_spec = pl.BlockSpec((2 * per, WIDTH, WIDTH), lambda g: (g, 0, 0))
    cols_spec = pl.BlockSpec((rows, TWO), lambda g: (0, g))
    full = lambda n, kind: jax.ShapeDtypeStruct((n, rows, WIDTH), kind)

    own, pay1, pay3, mrg = pl.pallas_call(
        functools.partial(lift_kernel, members, slots, levels, per, blocks),
        grid=(steps,),
        in_specs=[SMEM, SMEM, SMEM, ens_spec, pl.BlockSpec((slots, levels, TWO), lambda g: (0, 0, g)), loc_spec],
        out_specs=[cols_spec, one((8, rows, WIDTH)), one((12, rows, WIDTH)), one((4, rows, WIDTH))],
        out_shape=[jax.ShapeDtypeStruct((rows, columns), BF16), full(8, BF16), full(12, BF16), full(4, F32)],
        scratch_shapes=[
            pltpu.VMEM((rows, columns), BF16),
            pltpu.VMEM((columns, (DEV + SPAN) * WIDTH), BF16),
            pltpu.VMEM((2, WIDTH, WIDTH), BF16),
        ],
        compiler_params=params(32),
        name="lift",
    )(pairs, col_count, level_index, ens, control, loc_blocks)

    chips = [(i, (i + 1) % peers if i % 2 else (i - 1) % peers) for i in range(peers)]
    cores = [(i, i ^ 1) for i in range(peers)]
    r1 = lax.ppermute(pay1, "grid", chips)
    r3 = lax.ppermute(pay3, "grid", cores)

    acc, band = pl.pallas_call(
        functools.partial(near_kernel, per, blocks),
        grid=(steps,),
        in_specs=[SMEM, loc_spec, one((rows, columns))],
        out_specs=[one((rows, columns)), pl.BlockSpec((1, TWO, LANES), lambda g: (g, 0, 0))],
        out_shape=[jax.ShapeDtypeStruct((rows, columns), F32), jax.ShapeDtypeStruct((steps, TWO, LANES), BF16)],
        compiler_params=params(24),
        cost_estimate=pl.CostEstimate(flops=2 * 60 * rows * WIDTH * WIDTH, bytes_accessed=10 << 20, transcendentals=0),
        name="near",
    )(pairs, loc_blocks, own)

    pay1b = pl.pallas_call(
        merge_kernel,
        grid=(1,),
        in_specs=[SMEM, one((4, rows, WIDTH)), one((4, rows, WIDTH)),
                  pl.BlockSpec((4, rows, WIDTH), lambda g: (2, 0, 0))],
        out_specs=one((4, rows, WIDTH)),
        out_shape=full(4, BF16),
        compiler_params=params(12),
        name="merge",
    )(pairs, mrg, r3, r3)
    r1b = lax.ppermute(pay1b, "grid", chips)
    r3b = lax.ppermute(r1[:4], "grid", cores)

    acc = pl.pallas_call(
        far_kernel,
        grid=(steps,),
        in_specs=[SMEM, one((8, rows, WIDTH)), one((8, rows, WIDTH)),
                  pl.BlockSpec((1, TWO, LANES), lambda g: (g, 0, 0)), cols_spec],
        out_specs=cols_spec,
        out_shape=jax.ShapeDtypeStruct((rows, columns), F32),
        scratch_shapes=[pltpu.VMEM((rows, columns), BF16)],
        compiler_params=params(24),
        cost_estimate=pl.CostEstimate(flops=2 * 60 * rows * WIDTH * WIDTH, bytes_accessed=6 << 20, transcendentals=0),
        name="far",
    )(pairs, r1, r3, band, acc)

    two_blocks = pl.BlockSpec((2, rows, WIDTH), lambda g: (g, 0, 0))
    terms = pl.pallas_call(
        functools.partial(mix_kernel, members, slots, levels, members_all),
        grid=(steps,),
        in_specs=[SMEM, SMEM, ens_spec, cols_spec, pl.BlockSpec((1, TWO, 4 * WIDTH), lambda g: (g, 0, 3)),
                  two_blocks, two_blocks, one((4, rows, WIDTH)), one((4, rows, WIDTH))],
        out_specs=pl.BlockSpec((2, slots, levels, WIDTH), lambda g: (g, 0, 0, 0)),
        out_shape=jax.ShapeDtypeStruct((DEV, slots, levels, WIDTH), BF16),
        scratch_shapes=[pltpu.VMEM((rows, TWO), F32)],
        compiler_params=params(24),
        name="mix",
    )(pairs, col_count, ens, acc, band, r1, r3, r1b, r3b)
    parts = lax.all_to_all(terms, "mem", 0, 0, tiled=True)
    return jnp.sum(parts.astype(F32), axis=0)


def solution(mesh):
    return jax.shard_map(
        per_device,
        mesh=mesh,
        in_specs=(
            P("mem", None, None, "grid"),
            P(None, None, "grid"),
            P("grid"),
            P(),
            P("grid", None),
            P("grid", None, None),
        ),
        out_specs=P(None, None, ("grid", "mem")),
        check_vma=False,
    )
```

```python
import functools

import jax
import jax.numpy as jnp
from jax import lax
from jax.experimental import pallas as pl
from jax.experimental.pallas import tpu as pltpu
from jax.sharding import PartitionSpec as P

SPAN = 12
WIDTH = 128
DEV = 8
QUAD = 4 * WIDTH

vertical_scale = 8.0

F32 = jnp.float32
BF16 = jnp.bfloat16
VMEM = pl.BlockSpec(memory_space=pltpu.VMEM)
HBM = pl.BlockSpec(memory_space=pltpu.HBM)


def dot(a, b):
    return lax.dot_general(a, b, (((1,), (0,)), ((), ())), preferred_element_type=F32)


def dot_t(a, b):
    return lax.dot_general(a, b, (((1,), (1,)), ((), ())), preferred_element_type=F32)


def block(b):
    return slice(b * WIDTH, (b + 1) * WIDTH)


def by_core(first, second):
    odd = lax.rem(lax.axis_index("grid"), 2) == 1
    pl.when(jnp.logical_not(odd))(first)
    pl.when(odd)(second)


def lift_kernel(per, blocks, pairs_hbm, count_hbm, level_hbm, ens_hbm, control_hbm, loc_hbm,
                own_ref, band_ref, ens_ref, live_ref, pay1_ref,
                pairs_ref, count_ref, level_ref, control_ref, loc_ref, vert, sems):
    members, slots, levels, columns = ens_ref.shape
    group = WIDTH // levels
    cuts = [(m, min(group, members - m)) for m in range(0, members, group)]
    scalars = [
        pltpu.make_async_copy(level_hbm, level_ref, sems.at[0]),
        pltpu.make_async_copy(count_hbm, count_ref, sems.at[1]),
        pltpu.make_async_copy(pairs_hbm, pairs_ref, sems.at[2]),
    ]
    control_copy = pltpu.make_async_copy(control_hbm, control_ref, sems.at[3])
    ens_copies = [
        pltpu.make_async_copy(ens_hbm.at[pl.ds(m, n)], ens_ref.at[pl.ds(m, n)], sems.at[4 + i])
        for i, (m, n) in enumerate(cuts)
    ]
    some = 2 * per
    loc_copies = [
        pltpu.make_async_copy(loc_hbm.at[pl.ds(i * some, some)], loc_ref.at[pl.ds(i * some, some)], sems.at[8 + i])
        for i in range(DEV // 2)
    ]
    for copy in scalars + [control_copy] + ens_copies + loc_copies:
        copy.start()

    for i in range(DEV):
        low = i // 4 * 4
        for j in range(low, low + 16):
            if j < i or j > i + SPAN:
                band_ref[block(i), block(j)] = jnp.zeros((WIDTH, WIDTH), BF16)

    for copy in scalars:
        copy.wait()
    lane = lax.broadcasted_iota(jnp.int32, (levels, WIDTH), 1)
    row = lax.broadcasted_iota(jnp.int32, (levels, WIDTH), 0)
    by_lane = jnp.zeros((levels, WIDTH), F32)
    by_row = jnp.zeros((levels, WIDTH), F32)
    for l in range(levels):
        value = level_ref[l].astype(F32)
        by_lane = jnp.where(lane % levels == l, value, by_lane)
        by_row = jnp.where(row == l, value, by_row)
    v = jnp.exp(-jnp.abs(by_row - by_lane) / vertical_scale)
    for q in range(group):
        part = jnp.where(lane // levels == q, v, 0.0)
        high = part.astype(BF16)
        vert[0, q * levels:(q + 1) * levels, :] = high
        vert[1, q * levels:(q + 1) * levels, :] = (part - high.astype(F32)).astype(BF16)

    lane = lax.broadcasted_iota(jnp.int32, (DEV, WIDTH), 1)
    row = lax.broadcasted_iota(jnp.int32, (DEV, WIDTH), 0)
    limit = jnp.zeros((DEV, WIDTH), jnp.int32)
    for b in range(DEV):
        limit = jnp.where(row == b, count_ref[b], limit)
    live_ref[...] = (lane < limit).astype(F32)

    control_copy.wait()
    for b in range(DEV):
        control_ref[:, :, block(b)] = control_ref[:, :, block(b)] * live_ref[b:b + 1, :][None]

    for (m0, count), copy in zip(cuts, ens_copies):
        copy.wait()
        n = count * levels
        vh = vert[0, :n, :n]
        vl = vert[1, :n, :n]
        for c in range(0, columns, 2 * WIDTH):
            cols = slice(c, c + 2 * WIDTH)
            rows = []
            for m in range(m0, m0 + count):
                w = ens_ref[m, 0, :, cols].astype(F32) * control_ref[0, :, cols]
                for t in range(1, slots):
                    w = w + ens_ref[m, t, :, cols].astype(F32) * control_ref[t, :, cols]
                rows.append(w)
            w = jnp.concatenate(rows, axis=0)
            high = w.astype(BF16)
            low = (w - high.astype(F32)).astype(BF16)
            own_ref[m0 * levels:m0 * levels + n, cols] = (dot(vh, low) + dot(vl, high) + dot(vh, high)).astype(BF16)

    for i in range(DEV):
        if i % 2 == 0:
            loc_copies[i // 2].wait()
        left = SPAN * (SPAN + 1) // 2
        for p in range(i * per, (i + 1) * per):
            k = pairs_ref[1, p] - pairs_ref[0, p]
            k = jnp.where(k < 0, k + blocks, k)
            left = left - k
            band_ref[block(i), pl.ds(pl.multiple_of((i + k) * WIDTH, WIDTH), WIDTH)] = loc_ref[p]
        band_ref[block(i), pl.ds(pl.multiple_of((i + left) * WIDTH, WIDTH), WIDTH)] = jnp.zeros((WIDTH, WIDTH), BF16)

    def first():
        for b in range(DEV):
            pay1_ref[b] = own_ref[:, block(b)]

    def second():
        near = dot(own_ref[...], band_ref[:, 3 * QUAD:4 * QUAD]).astype(BF16)
        far = dot(own_ref[:, QUAD:], band_ref[QUAD:, 4 * QUAD:]).astype(BF16)
        for e in range(4):
            pay1_ref[e] = far[:, block(e)]
            pay1_ref[4 + e] = near[:, block(e)]

    by_core(first, second)


def reach_kernel(own_ref, band_ref, pay3_ref, mrg_ref):
    def first():
        for q in range(2, 5):
            start = QUAD if q == 4 else 0
            c = dot(own_ref[:, start:], band_ref[start:, q * QUAD:(q + 1) * QUAD]).astype(BF16)
            for e in range(4):
                pay3_ref[4 * (q - 2) + e] = c[:, block(e)]

    def second():
        c = dot(own_ref[...], band_ref[:, 2 * QUAD:3 * QUAD])
        for e in range(4):
            mrg_ref[e] = c[:, block(e)]
        for b in range(DEV):
            pay3_ref[b] = own_ref[:, block(b)]

    by_core(first, second)


def merge_kernel(mrg_ref, r3_ref, out_ref):
    def first():
        out_ref[...] = r3_ref[:4]

    def second():
        out_ref[...] = (mrg_ref[...] + r3_ref[8:].astype(F32)).astype(BF16)

    by_core(first, second)


def near_kernel(own_ref, band_ref, acc_ref, upper):
    for h in range(2):
        for i in range(4):
            for j in range(4):
                if j > i:
                    upper[h, block(i), block(j)] = band_ref[block(4 * h + i), block(4 * h + j)]
                else:
                    upper[h, block(i), block(j)] = jnp.zeros((WIDTH, WIDTH), BF16)
    acc_ref[:, :QUAD] = dot_t(own_ref[...], band_ref[:QUAD, :2 * QUAD])
    acc_ref[:, QUAD:] = dot_t(own_ref[:, QUAD:], band_ref[QUAD:, QUAD:2 * QUAD])
    acc_ref[:, :QUAD] += dot(own_ref[:, :QUAD], upper[0])
    acc_ref[:, QUAD:] += dot(own_ref[:, :QUAD], band_ref[:QUAD, QUAD:2 * QUAD])
    acc_ref[:, QUAD:] += dot(own_ref[:, QUAD:], upper[1])


def far_kernel(band_ref, acc_ref, r1_ref, r3_ref, out_ref, far):
    def first():
        for b in range(DEV):
            far[:, block(b)] = r3_ref[b]

    def second():
        for b in range(DEV):
            far[:, block(b)] = r1_ref[b]

    by_core(first, second)
    out_ref[...] = acc_ref[...] + dot_t(far[...], band_ref[:, 2 * QUAD:4 * QUAD])


def mix_kernel(members_all, ens_ref, band_ref, acc_ref, live_ref, r1_ref, r3_ref, r1b_ref, r3b_ref, out_ref,
               far, spread):
    members, slots, levels, columns = ens_ref.shape

    def first():
        for e in range(4):
            far[:, block(e)] = r3b_ref[e]
        for b in range(DEV):
            came = r1b_ref[b] if b < 4 else r1_ref[b]
            spread[:, block(b)] = acc_ref[:, block(b)] + came.astype(F32)

    def second():
        for e in range(4):
            far[:, block(e)] = r1b_ref[e]
        for b in range(DEV):
            came = r3_ref[b].astype(F32)
            if b < 4:
                came = came + r3b_ref[b].astype(F32)
            spread[:, block(b)] = acc_ref[:, block(b)] + came

    by_core(first, second)
    spread[:, QUAD:] += dot_t(far[...], band_ref[QUAD:, 4 * QUAD:])
    for b in range(DEV):
        totals = [jnp.zeros((levels, WIDTH), F32) for _ in range(slots)]
        for m in range(members):
            s = spread[m * levels:(m + 1) * levels, block(b)]
            for t in range(slots):
                totals[t] = totals[t] + ens_ref[m, t, :, block(b)].astype(F32) * s
        for t in range(slots):
            out_ref[b, t] = (totals[t] * live_ref[b:b + 1, :] / (members_all - 1)).astype(BF16)


def params(mib):
    return pltpu.CompilerParams(vmem_limit_bytes=mib << 20)


def per_device(ens, control, col_count, level_index, pair_blocks, loc_blocks):
    blocks_dev = col_count.shape[0]
    listed = pair_blocks.shape[0]
    per = listed // blocks_dev
    peers = lax.axis_size("grid")
    members, slots, levels, columns = ens.shape
    members_all = members * lax.axis_size("mem")
    rows = members * levels
    assert blocks_dev == DEV and columns == DEV * WIDTH and per == SPAN and peers % 2 == 0
    shape = jax.ShapeDtypeStruct
    pieces = lambda n, kind: shape((n, rows, WIDTH), kind)
    tie = lax.optimization_barrier

    args = (pair_blocks.T, col_count, level_index, ens, control, loc_blocks)
    own, band, ens_here, live, pay1 = pl.pallas_call(
        functools.partial(lift_kernel, per, peers * blocks_dev),
        in_specs=[HBM] * 6,
        out_specs=[VMEM] * 5,
        out_shape=[
            shape((rows, columns), BF16),
            shape((columns, (DEV + SPAN) * WIDTH), BF16),
            shape(ens.shape, BF16),
            shape((DEV, WIDTH), F32),
            pieces(8, BF16),
        ],
        scratch_shapes=[
            pltpu.SMEM((2, listed), jnp.int32),
            pltpu.SMEM(col_count.shape, jnp.int32),
            pltpu.SMEM(level_index.shape, jnp.int32),
            pltpu.VMEM(control.shape, F32),
            pltpu.VMEM(loc_blocks.shape, BF16),
            pltpu.VMEM((2, WIDTH, WIDTH), BF16),
            pltpu.SemaphoreType.DMA((12,)),
        ],
        compiler_params=params(28),
        name="lift",
    )(*[pltpu.with_memory_space_constraint(x, pltpu.HBM) for x in args])

    chips = [(i, (i + 1) % peers if i % 2 else (i - 1) % peers) for i in range(peers)]
    cores = [(i, i ^ 1) for i in range(peers)]
    r1 = lax.ppermute(pay1, "grid", chips)

    pay3, mrg = pl.pallas_call(
        reach_kernel,
        in_specs=[VMEM] * 2,
        out_specs=[VMEM] * 2,
        out_shape=[pieces(12, BF16), pieces(4, F32)],
        compiler_params=params(16),
        name="reach",
    )(own, band)
    r3 = lax.ppermute(pay3, "grid", cores)

    pay1b = pl.pallas_call(
        merge_kernel,
        in_specs=[VMEM] * 2,
        out_specs=VMEM,
        out_shape=pieces(4, BF16),
        compiler_params=params(12),
        name="merge",
    )(mrg, r3)
    r1b = lax.ppermute(pay1b, "grid", chips)

    own, pay1b = tie((own, pay1b))
    acc = pl.pallas_call(
        near_kernel,
        in_specs=[VMEM] * 2,
        out_specs=VMEM,
        out_shape=shape((rows, columns), F32),
        scratch_shapes=[pltpu.VMEM((2, QUAD, QUAD), BF16)],
        compiler_params=params(16),
        cost_estimate=pl.CostEstimate(flops=2 * 96 * rows * WIDTH * WIDTH, bytes_accessed=6 << 20, transcendentals=0),
        name="near",
    )(own, band)

    r1, acc = tie((r1, acc))
    r3b = lax.ppermute(r1[:4], "grid", cores)

    acc = pl.pallas_call(
        far_kernel,
        in_specs=[VMEM] * 4,
        out_specs=VMEM,
        out_shape=shape((rows, columns), F32),
        scratch_shapes=[pltpu.VMEM((rows, columns), BF16)],
        compiler_params=params(16),
        cost_estimate=pl.CostEstimate(flops=2 * 64 * rows * WIDTH * WIDTH, bytes_accessed=6 << 20, transcendentals=0),
        name="far",
    )(band, acc, r1, r3)

    terms = pl.pallas_call(
        functools.partial(mix_kernel, members_all),
        in_specs=[VMEM] * 8,
        out_specs=VMEM,
        out_shape=shape((DEV, slots, levels, WIDTH), BF16),
        scratch_shapes=[pltpu.VMEM((rows, QUAD), BF16), pltpu.VMEM((rows, columns), F32)],
        compiler_params=params(16),
        name="mix",
    )(ens_here, band, acc, live, r1, r3, r1b, r3b)
    parts = lax.all_to_all(terms, "mem", 0, 0, tiled=True)
    return jnp.sum(parts.astype(F32), axis=0)


def solution(mesh):
    return jax.shard_map(
        per_device,
        mesh=mesh,
        in_specs=(
            P("mem", None, None, "grid"),
            P(None, None, "grid"),
            P("grid"),
            P(),
            P("grid", None),
            P("grid", None, None),
        ),
        out_specs=P(None, None, ("grid", "mem")),
        check_vma=False,
    )
```

```python
import functools

import jax
import jax.numpy as jnp
from jax import lax
from jax.experimental import pallas as pl
from jax.experimental.pallas import tpu as pltpu
from jax.sharding import PartitionSpec as P

SPAN = 12
WIDTH = 128
DEV = 8
QUAD = 4 * WIDTH
ORDER = [4, 3, 2, 1, 0, 7, 6, 5]

vertical_scale = 8.0

F32 = jnp.float32
BF16 = jnp.bfloat16
VMEM = pl.BlockSpec(memory_space=pltpu.VMEM)
HBM = pl.BlockSpec(memory_space=pltpu.HBM)


def dot(a, b):
    return lax.dot_general(a, b, (((1,), (0,)), ((), ())), preferred_element_type=F32)


def dot_t(a, b):
    return lax.dot_general(a, b, (((1,), (1,)), ((), ())), preferred_element_type=F32)


def block(b):
    return slice(b * WIDTH, (b + 1) * WIDTH)


def by_core(first, second):
    odd = lax.rem(lax.axis_index("grid"), 2) == 1
    pl.when(jnp.logical_not(odd))(first)
    pl.when(odd)(second)


def lift_kernel(per, blocks, pairs_hbm, count_hbm, level_hbm, ens_hbm, control_hbm, loc_hbm,
                own_ref, band_ref, ens_ref, live_ref, pay1_ref, pay3_ref,
                pairs_ref, count_ref, level_ref, control_ref, loc_ref, vert, sems):
    members, slots, levels, columns = ens_ref.shape
    group = WIDTH // levels
    cuts = [(m, min(group, members - m)) for m in range(0, members, group)]
    scalars = [
        pltpu.make_async_copy(level_hbm, level_ref, sems.at[0]),
        pltpu.make_async_copy(count_hbm, count_ref, sems.at[1]),
        pltpu.make_async_copy(pairs_hbm, pairs_ref, sems.at[2]),
    ]
    control_copy = pltpu.make_async_copy(control_hbm, control_ref, sems.at[3])
    ens_copies = [
        pltpu.make_async_copy(ens_hbm.at[pl.ds(m, n)], ens_ref.at[pl.ds(m, n)], sems.at[4 + i])
        for i, (m, n) in enumerate(cuts)
    ]
    some = 2 * per
    loc_copies = [
        pltpu.make_async_copy(loc_hbm.at[pl.ds(i * some, some)], loc_ref.at[pl.ds(i * some, some)], sems.at[8 + i])
        for i in range(DEV // 2)
    ]
    for copy in scalars + [control_copy] + ens_copies + loc_copies:
        copy.start()

    for i in range(DEV):
        low = i // 4 * 4
        for j in range(low, low + 16):
            if j < i or j > i + SPAN:
                band_ref[block(i), block(j)] = jnp.zeros((WIDTH, WIDTH), BF16)

    for copy in scalars:
        copy.wait()
    lane = lax.broadcasted_iota(jnp.int32, (levels, WIDTH), 1)
    row = lax.broadcasted_iota(jnp.int32, (levels, WIDTH), 0)
    by_lane = jnp.zeros((levels, WIDTH), F32)
    by_row = jnp.zeros((levels, WIDTH), F32)
    for l in range(levels):
        value = level_ref[l].astype(F32)
        by_lane = jnp.where(lane % levels == l, value, by_lane)
        by_row = jnp.where(row == l, value, by_row)
    v = jnp.exp(-jnp.abs(by_row - by_lane) / vertical_scale)
    for q in range(group):
        part = jnp.where(lane // levels == q, v, 0.0)
        high = part.astype(BF16)
        vert[0, q * levels:(q + 1) * levels, :] = high
        vert[1, q * levels:(q + 1) * levels, :] = (part - high.astype(F32)).astype(BF16)

    lane = lax.broadcasted_iota(jnp.int32, (DEV, WIDTH), 1)
    row = lax.broadcasted_iota(jnp.int32, (DEV, WIDTH), 0)
    limit = jnp.zeros((DEV, WIDTH), jnp.int32)
    for b in range(DEV):
        limit = jnp.where(row == b, count_ref[b], limit)
    live_ref[...] = (lane < limit).astype(F32)

    control_copy.wait()
    for b in range(DEV):
        control_ref[:, :, block(b)] = control_ref[:, :, block(b)] * live_ref[b:b + 1, :][None]

    for (m0, count), copy in zip(cuts, ens_copies):
        copy.wait()
        n = count * levels
        vh = vert[0, :n, :n]
        vl = vert[1, :n, :n]
        for c in range(0, columns, 2 * WIDTH):
            cols = slice(c, c + 2 * WIDTH)
            rows = []
            for m in range(m0, m0 + count):
                w = ens_ref[m, 0, :, cols].astype(F32) * control_ref[0, :, cols]
                for t in range(1, slots):
                    w = w + ens_ref[m, t, :, cols].astype(F32) * control_ref[t, :, cols]
                rows.append(w)
            w = jnp.concatenate(rows, axis=0)
            high = w.astype(BF16)
            low = (w - high.astype(F32)).astype(BF16)
            own_ref[m0 * levels:m0 * levels + n, cols] = (dot(vh, low) + dot(vl, high) + dot(vh, high)).astype(BF16)

    for i in range(DEV):
        if i % 2 == 0:
            loc_copies[i // 2].wait()
        left = SPAN * (SPAN + 1) // 2
        for p in range(i * per, (i + 1) * per):
            k = pairs_ref[1, p] - pairs_ref[0, p]
            k = jnp.where(k < 0, k + blocks, k)
            left = left - k
            band_ref[block(i), pl.ds(pl.multiple_of((i + k) * WIDTH, WIDTH), WIDTH)] = loc_ref[p]
        band_ref[block(i), pl.ds(pl.multiple_of((i + left) * WIDTH, WIDTH), WIDTH)] = jnp.zeros((WIDTH, WIDTH), BF16)

    def first():
        for b in range(DEV):
            pay1_ref[b] = own_ref[:, block(b)]
        for q in range(2, 5):
            start = QUAD if q == 4 else 0
            c = dot(own_ref[:, start:], band_ref[start:, q * QUAD:(q + 1) * QUAD]).astype(BF16)
            for e in range(4):
                pay3_ref[4 * (q - 2) + e] = c[:, block(e)]

    def second():
        for b in range(DEV):
            pay3_ref[b] = own_ref[:, block(b)]
        near = dot(own_ref[...], band_ref[:, 3 * QUAD:4 * QUAD]).astype(BF16)
        far = dot(own_ref[:, QUAD:], band_ref[QUAD:, 4 * QUAD:]).astype(BF16)
        for e in range(4):
            pay1_ref[e] = far[:, block(e)]
            pay1_ref[4 + e] = near[:, block(e)]

    by_core(first, second)


def merge_kernel(own_ref, band_ref, r3_ref, out_ref):
    def first():
        out_ref[...] = r3_ref[:4]

    def second():
        c = dot(own_ref[...], band_ref[:, 2 * QUAD:3 * QUAD])
        for e in range(4):
            out_ref[e] = (c[:, block(e)] + r3_ref[8 + e].astype(F32)).astype(BF16)

    by_core(first, second)


def near_kernel(own_ref, band_ref, acc_ref, upper):
    for h in range(2):
        for i in range(4):
            for j in range(4):
                if j > i:
                    upper[h, block(i), block(j)] = band_ref[block(4 * h + i), block(4 * h + j)]
                else:
                    upper[h, block(i), block(j)] = jnp.zeros((WIDTH, WIDTH), BF16)
    acc_ref[:, :QUAD] = dot_t(own_ref[...], band_ref[:QUAD, :2 * QUAD])
    acc_ref[:, QUAD:] = dot_t(own_ref[:, QUAD:], band_ref[QUAD:, QUAD:2 * QUAD])
    acc_ref[:, :QUAD] += dot(own_ref[:, :QUAD], upper[0])
    acc_ref[:, QUAD:] += dot(own_ref[:, :QUAD], band_ref[:QUAD, QUAD:2 * QUAD])
    acc_ref[:, QUAD:] += dot(own_ref[:, QUAD:], upper[1])


def far_kernel(band_ref, acc_ref, r1_ref, r3_ref, out_ref, far):
    def first():
        for b in range(DEV):
            far[:, block(b)] = r3_ref[b]

    def second():
        for b in range(DEV):
            far[:, block(b)] = r1_ref[b]

    by_core(first, second)
    out_ref[...] = acc_ref[...] + dot_t(far[...], band_ref[:, 2 * QUAD:4 * QUAD])


def mix_kernel(members_all, ens_ref, band_ref, acc_ref, live_ref, r1_ref, r3_ref, r1b_ref, r3b_ref, out_ref,
               far, spread):
    members, slots, levels, columns = ens_ref.shape

    def first():
        for e in range(4):
            far[:, block(e)] = r3b_ref[e]
        for b in range(DEV):
            came = r1b_ref[b] if b < 4 else r1_ref[b]
            spread[:, block(b)] = acc_ref[:, block(b)] + came.astype(F32)

    def second():
        for e in range(4):
            far[:, block(e)] = r1b_ref[e]
        for b in range(DEV):
            came = r3_ref[b].astype(F32)
            if b < 4:
                came = came + r3b_ref[b].astype(F32)
            spread[:, block(b)] = acc_ref[:, block(b)] + came

    by_core(first, second)
    spread[:, QUAD:] += dot_t(far[...], band_ref[QUAD:, 4 * QUAD:])
    for b in range(DEV):
        totals = [jnp.zeros((levels, WIDTH), F32) for _ in range(slots)]
        for m in range(members):
            s = spread[m * levels:(m + 1) * levels, block(b)]
            for t in range(slots):
                totals[t] = totals[t] + ens_ref[m, t, :, block(b)].astype(F32) * s
        for t in range(slots):
            out_ref[ORDER.index(b), t] = (totals[t] * live_ref[b:b + 1, :] / (members_all - 1)).astype(BF16)


def params(mib):
    return pltpu.CompilerParams(vmem_limit_bytes=mib << 20)


def per_device(ens, control, col_count, level_index, pair_blocks, loc_blocks):
    blocks_dev = col_count.shape[0]
    listed = pair_blocks.shape[0]
    per = listed // blocks_dev
    peers = lax.axis_size("grid")
    members, slots, levels, columns = ens.shape
    members_all = members * lax.axis_size("mem")
    rows = members * levels
    assert blocks_dev == DEV and columns == DEV * WIDTH and per == SPAN and peers % 2 == 0
    shape = jax.ShapeDtypeStruct
    pieces = lambda n, kind: shape((n, rows, WIDTH), kind)
    tie = lax.optimization_barrier

    args = (pair_blocks.T, col_count, level_index, ens, control, loc_blocks)
    own, band, ens_here, live, pay1, pay3 = pl.pallas_call(
        functools.partial(lift_kernel, per, peers * blocks_dev),
        in_specs=[HBM] * 6,
        out_specs=[VMEM] * 6,
        out_shape=[
            shape((rows, columns), BF16),
            shape((columns, (DEV + SPAN) * WIDTH), BF16),
            shape(ens.shape, BF16),
            shape((DEV, WIDTH), F32),
            pieces(8, BF16),
            pieces(12, BF16),
        ],
        scratch_shapes=[
            pltpu.SMEM((2, listed), jnp.int32),
            pltpu.SMEM(col_count.shape, jnp.int32),
            pltpu.SMEM(level_index.shape, jnp.int32),
            pltpu.VMEM(control.shape, F32),
            pltpu.VMEM(loc_blocks.shape, BF16),
            pltpu.VMEM((2, WIDTH, WIDTH), BF16),
            pltpu.SemaphoreType.DMA((12,)),
        ],
        compiler_params=params(28),
        name="lift",
    )(*[pltpu.with_memory_space_constraint(x, pltpu.HBM) for x in args])

    chips = [(i, (i + 1) % peers if i % 2 else (i - 1) % peers) for i in range(peers)]
    cores = [(i, i ^ 1) for i in range(peers)]
    r1 = lax.ppermute(pay1, "grid", chips)

    r3 = lax.ppermute(pay3, "grid", cores)

    acc = pl.pallas_call(
        near_kernel,
        in_specs=[VMEM] * 2,
        out_specs=VMEM,
        out_shape=shape((rows, columns), F32),
        scratch_shapes=[pltpu.VMEM((2, QUAD, QUAD), BF16)],
        compiler_params=params(16),
        cost_estimate=pl.CostEstimate(flops=20000000000, bytes_accessed=100000000, transcendentals=0),
        name="near",
    )(own, band)

    r3, acc = tie((r3, acc))
    pay1b = pl.pallas_call(
        merge_kernel,
        in_specs=[VMEM] * 3,
        out_specs=VMEM,
        out_shape=pieces(4, BF16),
        compiler_params=params(12),
        cost_estimate=pl.CostEstimate(flops=1, bytes_accessed=1, transcendentals=0),
        name="merge",
    )(own, band, r3)
    r1b = lax.ppermute(pay1b, "grid", chips)

    r1, pay1b = tie((r1, pay1b))
    r3b = lax.ppermute(r1[:4], "grid", cores)

    acc = pl.pallas_call(
        far_kernel,
        in_specs=[VMEM] * 4,
        out_specs=VMEM,
        out_shape=shape((rows, columns), F32),
        scratch_shapes=[pltpu.VMEM((rows, columns), BF16)],
        compiler_params=params(16),
        cost_estimate=pl.CostEstimate(flops=4000000000, bytes_accessed=100000000, transcendentals=0),
        name="far",
    )(band, acc, r1, r3)

    terms = pl.pallas_call(
        functools.partial(mix_kernel, members_all),
        in_specs=[VMEM] * 8,
        out_specs=VMEM,
        out_shape=shape((DEV, slots, levels, WIDTH), BF16),
        scratch_shapes=[pltpu.VMEM((rows, QUAD), BF16), pltpu.VMEM((rows, columns), F32)],
        compiler_params=params(16),
        name="mix",
    )(ens_here, band, acc, live, r1, r3, r1b, r3b)
    parts = lax.all_to_all(terms, "mem", 0, 0, tiled=True, axis_index_groups=[ORDER])
    return jnp.sum(parts.astype(F32), axis=0)


def solution(mesh):
    return jax.shard_map(
        per_device,
        mesh=mesh,
        in_specs=(
            P("mem", None, None, "grid"),
            P(None, None, "grid"),
            P("grid"),
            P(),
            P("grid", None),
            P("grid", None, None),
        ),
        out_specs=P(None, None, ("grid", "mem")),
        check_vma=False,
    )
```

```python
import functools

import jax
import jax.numpy as jnp
from jax import lax
from jax.experimental import pallas as pl
from jax.experimental.pallas import tpu as pltpu
from jax.sharding import PartitionSpec as P

SPAN = 12
WIDTH = 128
DEV = 8
QUAD = 4 * WIDTH
ORDER = [4, 5, 3, 6, 2, 7, 1, 0]

vertical_scale = 8.0

F32 = jnp.float32
BF16 = jnp.bfloat16
VMEM = pl.BlockSpec(memory_space=pltpu.VMEM)
HBM = pl.BlockSpec(memory_space=pltpu.HBM)


def dot(a, b):
    return lax.dot_general(a, b, (((1,), (0,)), ((), ())), preferred_element_type=F32)


def dot_t(a, b):
    return lax.dot_general(a, b, (((1,), (1,)), ((), ())), preferred_element_type=F32)


def block(b):
    return slice(b * WIDTH, (b + 1) * WIDTH)


def by_core(first, second):
    odd = lax.rem(lax.axis_index("grid"), 2) == 1
    pl.when(jnp.logical_not(odd))(first)
    pl.when(odd)(second)


def lift_kernel(per, blocks, pairs_hbm, count_hbm, level_hbm, ens_hbm, control_hbm, loc_hbm,
                own_ref, band_ref, ens_ref, live_ref, pay1_ref, pay3_ref,
                pairs_ref, count_ref, level_ref, control_ref, loc_ref, vert, sems):
    members, slots, levels, columns = ens_ref.shape
    group = WIDTH // levels
    cuts = [(m, min(group, members - m)) for m in range(0, members, group)]
    scalars = [
        pltpu.make_async_copy(level_hbm, level_ref, sems.at[0]),
        pltpu.make_async_copy(count_hbm, count_ref, sems.at[1]),
        pltpu.make_async_copy(pairs_hbm, pairs_ref, sems.at[2]),
    ]
    control_copy = pltpu.make_async_copy(control_hbm, control_ref, sems.at[3])
    ens_copies = [
        pltpu.make_async_copy(ens_hbm.at[pl.ds(m, n)], ens_ref.at[pl.ds(m, n)], sems.at[4 + i])
        for i, (m, n) in enumerate(cuts)
    ]
    some = 2 * per
    loc_copies = [
        pltpu.make_async_copy(loc_hbm.at[pl.ds(i * some, some)], loc_ref.at[pl.ds(i * some, some)], sems.at[8 + i])
        for i in range(DEV // 2)
    ]
    for copy in scalars + [control_copy] + ens_copies + loc_copies:
        copy.start()

    for i in range(DEV):
        low = i // 4 * 4
        for j in range(low, low + 16):
            if j < i or j > i + SPAN:
                band_ref[block(i), block(j)] = jnp.zeros((WIDTH, WIDTH), BF16)

    for copy in scalars:
        copy.wait()
    lane = lax.broadcasted_iota(jnp.int32, (levels, WIDTH), 1)
    row = lax.broadcasted_iota(jnp.int32, (levels, WIDTH), 0)
    by_lane = jnp.zeros((levels, WIDTH), F32)
    by_row = jnp.zeros((levels, WIDTH), F32)
    for l in range(levels):
        value = level_ref[l].astype(F32)
        by_lane = jnp.where(lane % levels == l, value, by_lane)
        by_row = jnp.where(row == l, value, by_row)
    v = jnp.exp(-jnp.abs(by_row - by_lane) / vertical_scale)
    for q in range(group):
        part = jnp.where(lane // levels == q, v, 0.0)
        high = part.astype(BF16)
        vert[0, q * levels:(q + 1) * levels, :] = high
        vert[1, q * levels:(q + 1) * levels, :] = (part - high.astype(F32)).astype(BF16)

    lane = lax.broadcasted_iota(jnp.int32, (DEV, WIDTH), 1)
    row = lax.broadcasted_iota(jnp.int32, (DEV, WIDTH), 0)
    limit = jnp.zeros((DEV, WIDTH), jnp.int32)
    for b in range(DEV):
        limit = jnp.where(row == b, count_ref[b], limit)
    live_ref[...] = (lane < limit).astype(F32)

    control_copy.wait()
    for b in range(DEV):
        control_ref[:, :, block(b)] = control_ref[:, :, block(b)] * live_ref[b:b + 1, :][None]

    for (m0, count), copy in zip(cuts, ens_copies):
        copy.wait()
        n = count * levels
        vh = vert[0, :n, :n]
        vl = vert[1, :n, :n]
        for c in range(0, columns, 2 * WIDTH):
            cols = slice(c, c + 2 * WIDTH)
            rows = []
            for m in range(m0, m0 + count):
                w = ens_ref[m, 0, :, cols].astype(F32) * control_ref[0, :, cols]
                for t in range(1, slots):
                    w = w + ens_ref[m, t, :, cols].astype(F32) * control_ref[t, :, cols]
                rows.append(w)
            w = jnp.concatenate(rows, axis=0)
            high = w.astype(BF16)
            low = (w - high.astype(F32)).astype(BF16)
            own_ref[m0 * levels:m0 * levels + n, cols] = (dot(vh, low) + dot(vl, high) + dot(vh, high)).astype(BF16)

    for i in range(DEV):
        if i % 2 == 0:
            loc_copies[i // 2].wait()
        left = SPAN * (SPAN + 1) // 2
        for p in range(i * per, (i + 1) * per):
            k = pairs_ref[1, p] - pairs_ref[0, p]
            k = jnp.where(k < 0, k + blocks, k)
            left = left - k
            band_ref[block(i), pl.ds(pl.multiple_of((i + k) * WIDTH, WIDTH), WIDTH)] = loc_ref[p]
        band_ref[block(i), pl.ds(pl.multiple_of((i + left) * WIDTH, WIDTH), WIDTH)] = jnp.zeros((WIDTH, WIDTH), BF16)

    def first():
        for b in range(DEV):
            pay1_ref[b] = own_ref[:, block(b)]
        for q in range(2, 5):
            start = QUAD if q == 4 else 0
            c = dot(own_ref[:, start:], band_ref[start:, q * QUAD:(q + 1) * QUAD]).astype(BF16)
            for e in range(4):
                pay3_ref[4 * (q - 2) + e] = c[:, block(e)]

    def second():
        for b in range(DEV):
            pay3_ref[b] = own_ref[:, block(b)]
        near = dot(own_ref[...], band_ref[:, 3 * QUAD:4 * QUAD]).astype(BF16)
        far = dot(own_ref[:, QUAD:], band_ref[QUAD:, 4 * QUAD:]).astype(BF16)
        for e in range(4):
            pay1_ref[e] = far[:, block(e)]
            pay1_ref[4 + e] = near[:, block(e)]

    by_core(first, second)


def merge_kernel(own_ref, band_ref, r3_ref, out_ref):
    def first():
        out_ref[...] = r3_ref[:4]

    def second():
        c = dot(own_ref[...], band_ref[:, 2 * QUAD:3 * QUAD])
        for e in range(4):
            out_ref[e] = (c[:, block(e)] + r3_ref[8 + e].astype(F32)).astype(BF16)

    by_core(first, second)


def near_kernel(own_ref, band_ref, acc_ref, upper):
    for h in range(2):
        for i in range(4):
            for j in range(4):
                if j > i:
                    upper[h, block(i), block(j)] = band_ref[block(4 * h + i), block(4 * h + j)]
                else:
                    upper[h, block(i), block(j)] = jnp.zeros((WIDTH, WIDTH), BF16)
    acc_ref[:, :QUAD] = dot_t(own_ref[...], band_ref[:QUAD, :2 * QUAD])
    acc_ref[:, QUAD:] = dot_t(own_ref[:, QUAD:], band_ref[QUAD:, QUAD:2 * QUAD])
    acc_ref[:, :QUAD] += dot(own_ref[:, :QUAD], upper[0])
    acc_ref[:, QUAD:] += dot(own_ref[:, :QUAD], band_ref[:QUAD, QUAD:2 * QUAD])
    acc_ref[:, QUAD:] += dot(own_ref[:, QUAD:], upper[1])


def far_kernel(band_ref, acc_ref, r1_ref, r3_ref, out_ref, far):
    def first():
        for b in range(DEV):
            far[:, block(b)] = r3_ref[b]

    def second():
        for b in range(DEV):
            far[:, block(b)] = r1_ref[b]

    by_core(first, second)
    out_ref[...] = acc_ref[...] + dot_t(far[...], band_ref[:, 2 * QUAD:4 * QUAD])

    def first():
        for b in range(4, DEV):
            out_ref[:, block(b)] += r1_ref[b].astype(F32)

    def second():
        for b in range(DEV):
            out_ref[:, block(b)] += r3_ref[b].astype(F32)

    by_core(first, second)


def mix_kernel(members_all, ens_ref, band_ref, acc_ref, live_ref, r1b_ref, r3b_ref, out_ref, far, spread):
    members, slots, levels, columns = ens_ref.shape

    def take(lifted_ref, came_ref):
        for e in range(4):
            far[:, block(e)] = lifted_ref[e]
            spread[:, block(e)] = acc_ref[:, block(e)] + came_ref[e].astype(F32)

    by_core(lambda: take(r3b_ref, r1b_ref), lambda: take(r1b_ref, r3b_ref))
    spread[:, QUAD:] = acc_ref[:, QUAD:] + dot_t(far[...], band_ref[QUAD:, 4 * QUAD:])
    for b in range(DEV):
        totals = [jnp.zeros((levels, WIDTH), F32) for _ in range(slots)]
        for m in range(members):
            s = spread[m * levels:(m + 1) * levels, block(b)]
            for t in range(slots):
                totals[t] = totals[t] + ens_ref[m, t, :, block(b)].astype(F32) * s
        for t in range(slots):
            out_ref[ORDER.index(b), t] = (totals[t] * live_ref[b:b + 1, :] / (members_all - 1)).astype(BF16)


def params(mib):
    return pltpu.CompilerParams(vmem_limit_bytes=mib << 20)


def per_device(ens, control, col_count, level_index, pair_blocks, loc_blocks):
    blocks_dev = col_count.shape[0]
    listed = pair_blocks.shape[0]
    per = listed // blocks_dev
    peers = lax.axis_size("grid")
    members, slots, levels, columns = ens.shape
    members_all = members * lax.axis_size("mem")
    rows = members * levels
    assert blocks_dev == DEV and columns == DEV * WIDTH and per == SPAN and peers % 2 == 0
    shape = jax.ShapeDtypeStruct
    pieces = lambda n, kind: shape((n, rows, WIDTH), kind)
    tie = lax.optimization_barrier

    args = (pair_blocks.T, col_count, level_index, ens, control, loc_blocks)
    own, band, ens_here, live, pay1, pay3 = pl.pallas_call(
        functools.partial(lift_kernel, per, peers * blocks_dev),
        in_specs=[HBM] * 6,
        out_specs=[VMEM] * 6,
        out_shape=[
            shape((rows, columns), BF16),
            shape((columns, (DEV + SPAN) * WIDTH), BF16),
            shape(ens.shape, BF16),
            shape((DEV, WIDTH), F32),
            pieces(8, BF16),
            pieces(12, BF16),
        ],
        scratch_shapes=[
            pltpu.SMEM((2, listed), jnp.int32),
            pltpu.SMEM(col_count.shape, jnp.int32),
            pltpu.SMEM(level_index.shape, jnp.int32),
            pltpu.VMEM(control.shape, F32),
            pltpu.VMEM(loc_blocks.shape, BF16),
            pltpu.VMEM((2, WIDTH, WIDTH), BF16),
            pltpu.SemaphoreType.DMA((12,)),
        ],
        compiler_params=params(28),
        name="lift",
    )(*[pltpu.with_memory_space_constraint(x, pltpu.HBM) for x in args])

    chips = [(i, (i + 1) % peers if i % 2 else (i - 1) % peers) for i in range(peers)]
    cores = [(i, i ^ 1) for i in range(peers)]
    r1 = lax.ppermute(pay1, "grid", chips)

    r3 = lax.ppermute(pay3, "grid", cores)

    acc = pl.pallas_call(
        near_kernel,
        in_specs=[VMEM] * 2,
        out_specs=VMEM,
        out_shape=shape((rows, columns), F32),
        scratch_shapes=[pltpu.VMEM((2, QUAD, QUAD), BF16)],
        compiler_params=params(16),
        cost_estimate=pl.CostEstimate(flops=20000000000, bytes_accessed=100000000, transcendentals=0),
        name="near",
    )(own, band)

    r3, acc = tie((r3, acc))
    pay1b = pl.pallas_call(
        merge_kernel,
        in_specs=[VMEM] * 3,
        out_specs=VMEM,
        out_shape=pieces(4, BF16),
        compiler_params=params(12),
        cost_estimate=pl.CostEstimate(flops=1, bytes_accessed=1, transcendentals=0),
        name="merge",
    )(own, band, r3)
    r1b = lax.ppermute(pay1b, "grid", chips)

    r1, pay1b = tie((r1, pay1b))
    r3b = lax.ppermute(r1[:4], "grid", cores)

    acc = pl.pallas_call(
        far_kernel,
        in_specs=[VMEM] * 4,
        out_specs=VMEM,
        out_shape=shape((rows, columns), F32),
        scratch_shapes=[pltpu.VMEM((rows, columns), BF16)],
        compiler_params=params(16),
        cost_estimate=pl.CostEstimate(flops=4000000000, bytes_accessed=100000000, transcendentals=0),
        name="far",
    )(band, acc, r1, r3)

    terms = pl.pallas_call(
        functools.partial(mix_kernel, members_all),
        in_specs=[VMEM] * 6,
        out_specs=VMEM,
        out_shape=shape((DEV, slots, levels, WIDTH), BF16),
        scratch_shapes=[pltpu.VMEM((rows, QUAD), BF16), pltpu.VMEM((rows, columns), F32)],
        compiler_params=params(16),
        name="mix",
    )(ens_here, band, acc, live, r1b, r3b)
    parts = lax.all_to_all(terms, "mem", 0, 0, tiled=True, axis_index_groups=[ORDER])
    return jnp.sum(parts.astype(F32), axis=0)


def solution(mesh):
    return jax.shard_map(
        per_device,
        mesh=mesh,
        in_specs=(
            P("mem", None, None, "grid"),
            P(None, None, "grid"),
            P("grid"),
            P(),
            P("grid", None),
            P("grid", None, None),
        ),
        out_specs=P(None, None, ("grid", "mem")),
        check_vma=False,
    )
```

```python
import functools

import jax
import jax.numpy as jnp
from jax import lax
from jax.experimental import pallas as pl
from jax.experimental.pallas import tpu as pltpu
from jax.sharding import PartitionSpec as P

SPAN = 12
WIDTH = 128
DEV = 8
QUAD = 4 * WIDTH
ORDER = [4, 5, 3, 6, 2, 7, 1, 0]

vertical_scale = 8.0

F32 = jnp.float32
BF16 = jnp.bfloat16
VMEM = pl.BlockSpec(memory_space=pltpu.VMEM)
HBM = pl.BlockSpec(memory_space=pltpu.HBM)


def dot(a, b):
    return lax.dot_general(a, b, (((1,), (0,)), ((), ())), preferred_element_type=F32)


def dot_t(a, b):
    return lax.dot_general(a, b, (((1,), (1,)), ((), ())), preferred_element_type=F32)


def block(b):
    return slice(b * WIDTH, (b + 1) * WIDTH)


def by_core(first, second):
    odd = lax.rem(lax.axis_index("grid"), 2) == 1
    pl.when(jnp.logical_not(odd))(first)
    pl.when(odd)(second)


def lift_kernel(per, blocks, pairs_hbm, count_hbm, level_hbm, ens_hbm, control_hbm, loc_hbm,
                own_ref, band_ref, ens_ref, live_ref, pay1_ref, pay3_ref,
                pairs_ref, count_ref, level_ref, control_ref, loc_ref, vert, sems):
    members, slots, levels, columns = ens_ref.shape
    group = WIDTH // levels
    cuts = [(m, min(group, members - m)) for m in range(0, members, group)]
    scalars = [
        pltpu.make_async_copy(level_hbm, level_ref, sems.at[0]),
        pltpu.make_async_copy(count_hbm, count_ref, sems.at[1]),
        pltpu.make_async_copy(pairs_hbm, pairs_ref, sems.at[2]),
    ]
    control_copy = pltpu.make_async_copy(control_hbm, control_ref, sems.at[3])
    ens_copies = [
        pltpu.make_async_copy(ens_hbm.at[pl.ds(m, n)], ens_ref.at[pl.ds(m, n)], sems.at[4 + i])
        for i, (m, n) in enumerate(cuts)
    ]
    some = 2 * per
    loc_copies = [
        pltpu.make_async_copy(loc_hbm.at[pl.ds(i * some, some)], loc_ref.at[pl.ds(i * some, some)], sems.at[8 + i])
        for i in range(DEV // 2)
    ]
    for copy in scalars + [control_copy] + ens_copies + loc_copies:
        copy.start()

    for i in range(DEV):
        low = i // 4 * 4
        for j in range(low, low + 16):
            if j < i or j > i + SPAN:
                band_ref[block(i), block(j)] = jnp.zeros((WIDTH, WIDTH), BF16)

    for copy in scalars:
        copy.wait()
    lane = lax.broadcasted_iota(jnp.int32, (levels, WIDTH), 1)
    row = lax.broadcasted_iota(jnp.int32, (levels, WIDTH), 0)
    by_lane = jnp.zeros((levels, WIDTH), F32)
    by_row = jnp.zeros((levels, WIDTH), F32)
    for l in range(levels):
        value = level_ref[l].astype(F32)
        by_lane = jnp.where(lane % levels == l, value, by_lane)
        by_row = jnp.where(row == l, value, by_row)
    v = jnp.exp(-jnp.abs(by_row - by_lane) / vertical_scale)
    for q in range(group):
        part = jnp.where(lane // levels == q, v, 0.0)
        high = part.astype(BF16)
        vert[0, q * levels:(q + 1) * levels, :] = high
        vert[1, q * levels:(q + 1) * levels, :] = (part - high.astype(F32)).astype(BF16)

    lane = lax.broadcasted_iota(jnp.int32, (DEV, WIDTH), 1)
    row = lax.broadcasted_iota(jnp.int32, (DEV, WIDTH), 0)
    limit = jnp.zeros((DEV, WIDTH), jnp.int32)
    for b in range(DEV):
        limit = jnp.where(row == b, count_ref[b], limit)
    live_ref[...] = (lane < limit).astype(F32)

    control_copy.wait()
    for b in range(DEV):
        control_ref[:, :, block(b)] = control_ref[:, :, block(b)] * live_ref[b:b + 1, :][None]

    for (m0, count), copy in zip(cuts, ens_copies):
        copy.wait()
        n = count * levels
        vh = vert[0, :n, :n]
        vl = vert[1, :n, :n]
        vv = jnp.concatenate([vh, vh], axis=1)
        for c in range(0, columns, 2 * WIDTH):
            cols = slice(c, c + 2 * WIDTH)
            rows = []
            for m in range(m0, m0 + count):
                w = ens_ref[m, 0, :, cols].astype(F32) * control_ref[0, :, cols]
                for t in range(1, slots):
                    w = w + ens_ref[m, t, :, cols].astype(F32) * control_ref[t, :, cols]
                rows.append(w)
            w = jnp.concatenate(rows, axis=0)
            high = w.astype(BF16)
            low = (w - high.astype(F32)).astype(BF16)
            both = jnp.concatenate([high, low], axis=0)
            own_ref[m0 * levels:m0 * levels + n, cols] = (dot(vl, high) + dot(vv, both)).astype(BF16)

    for i in range(DEV):
        if i % 2 == 0:
            loc_copies[i // 2].wait()
        left = SPAN * (SPAN + 1) // 2
        for p in range(i * per, (i + 1) * per):
            k = pairs_ref[1, p] - pairs_ref[0, p]
            k = jnp.where(k < 0, k + blocks, k)
            left = left - k
            band_ref[block(i), pl.ds(pl.multiple_of((i + k) * WIDTH, WIDTH), WIDTH)] = loc_ref[p]
        band_ref[block(i), pl.ds(pl.multiple_of((i + left) * WIDTH, WIDTH), WIDTH)] = jnp.zeros((WIDTH, WIDTH), BF16)

    def first():
        for b in range(DEV):
            pay1_ref[b] = own_ref[:, block(b)]
        for q in range(2, 5):
            start = QUAD if q == 4 else 0
            c = dot(own_ref[:, start:], band_ref[start:, q * QUAD:(q + 1) * QUAD]).astype(BF16)
            for e in range(4):
                pay3_ref[4 * (q - 2) + e] = c[:, block(e)]

    def second():
        for b in range(DEV):
            pay3_ref[b] = own_ref[:, block(b)]
        near = dot(own_ref[...], band_ref[:, 3 * QUAD:4 * QUAD]).astype(BF16)
        far = dot(own_ref[:, QUAD:], band_ref[QUAD:, 4 * QUAD:]).astype(BF16)
        for e in range(4):
            pay1_ref[e] = far[:, block(e)]
            pay1_ref[4 + e] = near[:, block(e)]

    by_core(first, second)


def merge_kernel(own_ref, band_ref, r3_ref, out_ref):
    def first():
        out_ref[...] = r3_ref[:4]

    def second():
        c = dot(own_ref[...], band_ref[:, 2 * QUAD:3 * QUAD])
        for e in range(4):
            out_ref[e] = (c[:, block(e)] + r3_ref[8 + e].astype(F32)).astype(BF16)

    by_core(first, second)


def near_kernel(own_ref, band_ref, acc_ref, upper):
    for h in range(2):
        for i in range(4):
            for j in range(4):
                if j > i:
                    upper[h, block(i), block(j)] = band_ref[block(4 * h + i), block(4 * h + j)]
                else:
                    upper[h, block(i), block(j)] = jnp.zeros((WIDTH, WIDTH), BF16)
    acc_ref[:, :QUAD] = dot_t(own_ref[...], band_ref[:QUAD, :2 * QUAD])
    acc_ref[:, QUAD:] = dot_t(own_ref[:, QUAD:], band_ref[QUAD:, QUAD:2 * QUAD])
    acc_ref[:, :QUAD] += dot(own_ref[:, :QUAD], upper[0])
    acc_ref[:, QUAD:] += dot(own_ref[:, :QUAD], band_ref[:QUAD, QUAD:2 * QUAD])
    acc_ref[:, QUAD:] += dot(own_ref[:, QUAD:], upper[1])


def far_kernel(band_ref, acc_ref, r1_ref, r3_ref, out_ref, far):
    def first():
        for b in range(DEV):
            far[:, block(b)] = r3_ref[b]

    def second():
        for b in range(DEV):
            far[:, block(b)] = r1_ref[b]

    by_core(first, second)
    out_ref[...] = acc_ref[...] + dot_t(far[...], band_ref[:, 2 * QUAD:4 * QUAD])

    def first():
        for b in range(4, DEV):
            out_ref[:, block(b)] += r1_ref[b].astype(F32)

    def second():
        for b in range(DEV):
            out_ref[:, block(b)] += r3_ref[b].astype(F32)

    by_core(first, second)


def mix_kernel(members_all, ens_ref, band_ref, acc_ref, live_ref, r1b_ref, r3b_ref, out_ref, far, spread):
    members, slots, levels, columns = ens_ref.shape

    def take(lifted_ref, came_ref):
        for e in range(4):
            far[:, block(e)] = lifted_ref[e]
            spread[:, block(e)] = acc_ref[:, block(e)] + came_ref[e].astype(F32)

    by_core(lambda: take(r3b_ref, r1b_ref), lambda: take(r1b_ref, r3b_ref))
    spread[:, QUAD:] = acc_ref[:, QUAD:] + dot_t(far[...], band_ref[QUAD:, 4 * QUAD:])
    for b in range(DEV):
        totals = [jnp.zeros((levels, WIDTH), F32) for _ in range(slots)]
        for m in range(members):
            s = spread[m * levels:(m + 1) * levels, block(b)]
            for t in range(slots):
                totals[t] = totals[t] + ens_ref[m, t, :, block(b)].astype(F32) * s
        for t in range(slots):
            out_ref[ORDER.index(b), t] = (totals[t] * live_ref[b:b + 1, :] / (members_all - 1)).astype(BF16)


def params(mib):
    return pltpu.CompilerParams(vmem_limit_bytes=mib << 20)


def per_device(ens, control, col_count, level_index, pair_blocks, loc_blocks):
    blocks_dev = col_count.shape[0]
    listed = pair_blocks.shape[0]
    per = listed // blocks_dev
    peers = lax.axis_size("grid")
    members, slots, levels, columns = ens.shape
    members_all = members * lax.axis_size("mem")
    rows = members * levels
    assert blocks_dev == DEV and columns == DEV * WIDTH and per == SPAN and peers % 2 == 0
    shape = jax.ShapeDtypeStruct
    pieces = lambda n, kind: shape((n, rows, WIDTH), kind)
    tie = lax.optimization_barrier

    args = (pair_blocks.T, col_count, level_index, ens, control, loc_blocks)
    own, band, ens_here, live, pay1, pay3 = pl.pallas_call(
        functools.partial(lift_kernel, per, peers * blocks_dev),
        in_specs=[HBM] * 6,
        out_specs=[VMEM] * 6,
        out_shape=[
            shape((rows, columns), BF16),
            shape((columns, (DEV + SPAN) * WIDTH), BF16),
            shape(ens.shape, BF16),
            shape((DEV, WIDTH), F32),
            pieces(8, BF16),
            pieces(12, BF16),
        ],
        scratch_shapes=[
            pltpu.SMEM((2, listed), jnp.int32),
            pltpu.SMEM(col_count.shape, jnp.int32),
            pltpu.SMEM(level_index.shape, jnp.int32),
            pltpu.VMEM(control.shape, F32),
            pltpu.VMEM(loc_blocks.shape, BF16),
            pltpu.VMEM((2, WIDTH, WIDTH), BF16),
            pltpu.SemaphoreType.DMA((12,)),
        ],
        compiler_params=params(28),
        name="lift",
    )(*[pltpu.with_memory_space_constraint(x, pltpu.HBM) for x in args])

    chips = [(i, (i + 1) % peers if i % 2 else (i - 1) % peers) for i in range(peers)]
    cores = [(i, i ^ 1) for i in range(peers)]
    r1 = lax.ppermute(pay1, "grid", chips)

    r3 = lax.ppermute(pay3, "grid", cores)

    acc = pl.pallas_call(
        near_kernel,
        in_specs=[VMEM] * 2,
        out_specs=VMEM,
        out_shape=shape((rows, columns), F32),
        scratch_shapes=[pltpu.VMEM((2, QUAD, QUAD), BF16)],
        compiler_params=params(16),
        cost_estimate=pl.CostEstimate(flops=20000000000, bytes_accessed=100000000, transcendentals=0),
        name="near",
    )(own, band)

    r3, acc = tie((r3, acc))
    pay1b = pl.pallas_call(
        merge_kernel,
        in_specs=[VMEM] * 3,
        out_specs=VMEM,
        out_shape=pieces(4, BF16),
        compiler_params=params(12),
        cost_estimate=pl.CostEstimate(flops=1, bytes_accessed=1, transcendentals=0),
        name="merge",
    )(own, band, r3)
    r1b = lax.ppermute(pay1b, "grid", chips)

    r1, pay1b = tie((r1, pay1b))
    r3b = lax.ppermute(r1[:4], "grid", cores)

    acc = pl.pallas_call(
        far_kernel,
        in_specs=[VMEM] * 4,
        out_specs=VMEM,
        out_shape=shape((rows, columns), F32),
        scratch_shapes=[pltpu.VMEM((rows, columns), BF16)],
        compiler_params=params(16),
        cost_estimate=pl.CostEstimate(flops=4000000000, bytes_accessed=100000000, transcendentals=0),
        name="far",
    )(band, acc, r1, r3)

    terms = pl.pallas_call(
        functools.partial(mix_kernel, members_all),
        in_specs=[VMEM] * 6,
        out_specs=VMEM,
        out_shape=shape((DEV, slots, levels, WIDTH), BF16),
        scratch_shapes=[pltpu.VMEM((rows, QUAD), BF16), pltpu.VMEM((rows, columns), F32)],
        compiler_params=params(16),
        name="mix",
    )(ens_here, band, acc, live, r1b, r3b)
    parts = lax.all_to_all(terms, "mem", 0, 0, tiled=True, axis_index_groups=[ORDER])
    return jnp.sum(parts.astype(F32), axis=0)


def solution(mesh):
    return jax.shard_map(
        per_device,
        mesh=mesh,
        in_specs=(
            P("mem", None, None, "grid"),
            P(None, None, "grid"),
            P("grid"),
            P(),
            P("grid", None),
            P("grid", None, None),
        ),
        out_specs=P(None, None, ("grid", "mem")),
        check_vma=False,
    )
```
